512 devices in a mesh: tile: 32 (over z, core), mem: 16 (over y, x).
Axes of the slice: x: 4, y: 4, z: 16, core: 2. Of those that a mesh axis runs over, the one named last changes fastest.
Arguments:
- prior_ensemble: bfloat16 [256, 1048576], P('mem', 'tile'), may hold values from -6 to 6
- measurement_anomaly_matrix: bfloat16 [257, 2097152], P(None, ('tile', 'mem')), may hold values from -15 to 15, as said below
- measured_per_portion: int32 [512], replicated, may hold values from 1 to 4096, as said below
- locality_support_marks: int32 [3, 16384], replicated, may hold values 0 or 1
Outputs:
- analysis: bfloat16 [256, 1048576], P(None, ('tile', 'mem'))
The draws below stay inside these ranges and needn't reach their ends.
Inputs may be any that keep to these rules, and one draw needn't show every extreme that they name: `measurement_anomaly_matrix`: scaled perturbations and innovations of real value; slots past a shard's count are padding. `measured_per_portion`: shard g holds slots g * 4096 to (g + 1) * 4096 - 1 of the whole, its live ones first; some shard is full in every draw.
All inputs are finite; a program needn't handle non-finite values. Where the reference program divides by a largest or mean magnitude, that divisor is 1e-20 or more.
Results may differ from the reference program's by a relative error of at most 0.0061.
Values may be sent and summed in bfloat16 or wider, within the bound.
A program may use at most 64 MiB of HBM per device.

```python
import math
import jax
import jax.numpy as jnp
from jax import lax

ENSEMBLE_WIDTH = 256
OBS_DEV = 4096
NS_STEPS = 8
K1 = 257
PATCH_LENGTH = 32768
DOMAIN_LENGTH = 1048576
OBS_T = 65536
NOBS = 2097152
GROUPS = 512
N_TILE = 32
N_MEM = 16


def draw_measurement_anomaly_matrix(key, part):
    key = jax.random.fold_in(key, 7)
    keys = jax.random.split(key, 4)
    noise = jnp.clip(jax.random.normal(keys[0], (ENSEMBLE_WIDTH, NOBS), jnp.float32), -6.0, 6.0)
    innovation = 3.0 * jnp.clip(jax.random.normal(keys[3], (1, NOBS), jnp.float32), -5.0, 5.0)
    member_scale = jnp.exp(jax.random.uniform(keys[1], (ENSEMBLE_WIDTH, 1), jnp.float32, 0.0, math.log(100.0)))
    site_scale = jnp.exp(jax.random.uniform(keys[2], (1, NOBS), jnp.float32, 0.0, math.log(3.0)))
    base_scale = (ENSEMBLE_WIDTH / (64.0 * OBS_T)) ** 0.5
    perturbed = jnp.clip(base_scale * member_scale * site_scale * noise, -15.0, 15.0)
    return jnp.concatenate([perturbed, innovation], axis=0).astype(jnp.bfloat16)


def draw_measured_per_portion(key, part):
    key = jax.random.fold_in(key, 13)
    keys = jax.random.split(key, 3)
    first_draw = jax.random.randint(keys[0], (GROUPS,), 1, OBS_DEV + 1)
    second_draw = jax.random.randint(keys[1], (GROUPS,), 1, OBS_DEV + 1)
    counts = jnp.maximum(first_draw * second_draw // OBS_DEV, 1)
    busiest = jax.random.randint(keys[2], (), 0, GROUPS)
    return jnp.where(jnp.arange(GROUPS) == busiest, OBS_DEV, counts).astype(jnp.int32)


def with_ends(array, key, smallest, largest):
    index_at = [jax.random.randint(jax.random.fold_in(key, axis), (), 0, length) for axis, length in enumerate(array.shape)]
    longest = array.shape.index(max(array.shape))
    neighbour = index_at[:longest] + [(index_at[longest] + 1) % array.shape[longest]] + index_at[longest + 1:]
    return array.at[tuple(index_at)].set(smallest).at[tuple(neighbour)].set(largest)


def levels(rng, shape, shards, smallest, high):
    gain = 1.0
    for axis_at, shards_of in shards:
        steps = jax.random.uniform(jax.random.fold_in(jax.random.fold_in(rng, 6), axis_at), (shards_of,), jnp.float32, smallest / len(shards), high / len(shards))
        gain = gain * jnp.repeat(jnp.exp(steps), shape[axis_at] // shards_of).reshape((-1,) + (1,) * (len(shape) - 1 - axis_at))
    return gain


def bell_draw(rng, extent, deviation, bound, cuts=(), kind=jnp.bfloat16):
    level = levels(rng, extent, cuts, -0.22, 0.18) if cuts else 1.0
    values = jax.random.normal(rng, extent, jnp.float32) * deviation * level
    return jnp.minimum(jnp.maximum(values, -bound), bound).astype(kind)


def setup_inputs(seed: int = 0) -> dict:
    splits = jax.random.split(jax.random.key(seed), 5)
    return {
        "prior_ensemble": bell_draw(splits[0], (ENSEMBLE_WIDTH, DOMAIN_LENGTH), 1.0, 6.0, ((0, 16), (1, 32))),
        "measurement_anomaly_matrix": draw_measurement_anomaly_matrix(jax.random.fold_in(splits[4], 71), 0),
        "measured_per_portion": draw_measured_per_portion(jax.random.fold_in(splits[4], 71), 0),
        "locality_support_marks": with_ends((jax.random.randint(splits[3], (3, NOBS // 128), 0, 4) < 3).astype(jnp.int32), jax.random.fold_in(splits[3], 1), 0, 1),
    }


loc_width = 1.0

def tile_weights(locality_support_marks, measured_per_portion, source_tile, offset):
    slot_index = jnp.arange(OBS_T, dtype=jnp.int32)
    owner = source_tile * N_MEM + slot_index // OBS_DEV
    alive_mask = slot_index % OBS_DEV < measured_per_portion[owner]
    pattern_rows = locality_support_marks[offset][(source_tile * OBS_T + slot_index) // 128]
    position = (slot_index.astype(jnp.float32) + 0.5) / OBS_T
    distance = offset - 1 + position - 0.5
    smooth = jnp.exp(-0.5 * (distance / loc_width) * (distance / loc_width))
    return jnp.where(alive_mask & (pattern_rows > 0), smooth, jnp.zeros_like(smooth))

def mixing_matrix(products, members):
    gram_block = products[:members, :members]
    drive_vector = products[:members, members]
    identity = jnp.eye(members, dtype=jnp.float32)
    system = (members - 1.0) * identity + gram_block
    bound_scale = jnp.max(lax.optimization_barrier(jnp.sum(jnp.abs(system), axis=1)))
    iterate = system / bound_scale
    inverse_root = identity
    for sweep_index in range(NS_STEPS):
        factor = 1.5 * identity - 0.5 * jnp.dot(inverse_root, iterate, precision=lax.Precision.HIGHEST)
        iterate = jnp.dot(iterate, factor, precision=lax.Precision.HIGHEST)
        inverse_root = jnp.dot(factor, inverse_root, precision=lax.Precision.HIGHEST)
    root_inverse = inverse_root / jnp.sqrt(bound_scale)
    mean_shift = jnp.dot(root_inverse, jnp.dot(root_inverse, drive_vector, precision=lax.Precision.HIGHEST), precision=lax.Precision.HIGHEST)
    weights = jnp.sqrt(members - 1.0) * root_inverse.T + mean_shift[None, :]
    mixing = weights + (1.0 - lax.optimization_barrier(jnp.sum(weights, axis=1)))[:, None] / members
    return mixing.astype(jnp.bfloat16)

def reference(prior_ensemble, measurement_anomaly_matrix, measured_per_portion, locality_support_marks):
    shaped_obs = measurement_anomaly_matrix.reshape(K1, N_TILE, OBS_T)
    patchwise_model_matrix = prior_ensemble.reshape(ENSEMBLE_WIDTH, N_TILE, PATCH_LENGTH)

    def one_tile(tile_index):
        products = jnp.zeros((K1, K1), jnp.float32)
        for offset in range(3):
            source_tile = ((tile_index + offset - 1 + N_TILE) % N_TILE).astype(jnp.int32)
            columns = jnp.take(shaped_obs, source_tile, axis=1)
            root_weight = tile_weights(locality_support_marks, measured_per_portion, source_tile, offset)
            scaled = (columns.astype(jnp.float32) * root_weight[None, :]).astype(jnp.bfloat16)
            products = products + jnp.dot(scaled, scaled.T, preferred_element_type=jnp.float32)
        mixing = mixing_matrix(products, ENSEMBLE_WIDTH)
        state_cols = jnp.take(patchwise_model_matrix, tile_index, axis=1)
        return jnp.dot(mixing, state_cols, preferred_element_type=jnp.float32).astype(jnp.bfloat16)
    result = lax.map(one_tile, jnp.arange(N_TILE, dtype=jnp.int32))
    return jnp.transpose(result, (1, 0, 2)).reshape(ENSEMBLE_WIDTH, DOMAIN_LENGTH)
```

```python
import functools

import jax
import jax.numpy as jnp
from jax import lax
from jax.experimental import pallas as pl
from jax.experimental.pallas import tpu as pltpu
from jax.sharding import PartitionSpec as P

MESH = pl.DeviceIdType.MESH
NS_STEPS = 8
LANES = 128
CHUNKS = 4


def split(x):
    high = x.astype(jnp.bfloat16)
    return high, (x - high.astype(jnp.float32)).astype(jnp.bfloat16)


def product(left, right):
    (lh, ll), (rh, rl) = left, right
    return jnp.dot(
        jnp.concatenate([lh, ll, lh], axis=1),
        jnp.concatenate([rh, rh, rl], axis=0),
        preferred_element_type=jnp.float32,
    )


def kernel(
    n_tile,
    n_mem,
    counts,
    prior,
    obs,
    marks,
    mixing_out,
    gathered,
    obs_v,
    marks_v,
    marks_t,
    weight_v,
    scaled_v,
    cross_out,
    inner_out,
    cross_in,
    inner_in,
    total,
    parts_in,
    system_v,
    local_sem,
    obs_sem,
    pair_send,
    pair_recv,
    rs_send,
    rs_recv,
    ag_send,
    ag_recv,
    a2a_send,
    a2a_recv,
):
    tile = lax.axis_index("tile")
    mem = lax.axis_index("mem")
    members = mixing_out.shape[0]
    half = members // 2
    obs_dev = obs.shape[1]
    blocks = obs_dev // LANES
    part = half // n_mem
    own_rows = prior.shape[0]
    own_cols = gathered.shape[1]

    cross_offset = 1 - 2 * lax.rem(tile, 2)
    cross_tile = lax.rem(tile - cross_offset + n_tile, n_tile)
    inner_tile = lax.rem(tile + cross_offset + n_tile, n_tile)
    peers = [lax.rem(mem + k, n_mem) for k in range(1, n_mem)]

    first_block = (tile * n_mem + mem) * blocks
    aligned = pl.multiple_of((first_block // LANES) * LANES, LANES)
    inside = pl.multiple_of(lax.rem(first_block, LANES), blocks)
    marks_copy = pltpu.make_async_copy(
        marks.at[:, pl.ds(aligned, LANES)], marks_v, local_sem.at[0]
    )
    marks_copy.start()
    width = obs_dev // CHUNKS
    obs_copies = [
        pltpu.make_async_copy(
            obs.at[:, pl.ds(c * width, width)], obs_v.at[:, pl.ds(c * width, width)], obs_sem.at[c]
        )
        for c in range(CHUNKS)
    ]
    for copy in obs_copies:
        copy.start()

    barrier = pltpu.get_barrier_semaphore()
    for other in (cross_tile, inner_tile):
        pl.semaphore_signal(barrier, inc=1, device_id=(other, mem), device_id_type=MESH)
    for peer in peers:
        pl.semaphore_signal(barrier, inc=1, device_id=(tile, peer), device_id_type=MESH)

    marks_copy.wait()
    alive_count = counts[tile * n_mem + mem]
    slot = (
        lax.broadcasted_iota(jnp.int32, (blocks, LANES), 0) * LANES
        + lax.broadcasted_iota(jnp.int32, (blocks, LANES), 1)
    )
    alive = slot < alive_count
    position = ((mem * obs_dev + slot).astype(jnp.float32) + 0.5) / (obs_dev * n_mem)
    offsets = (cross_offset, -cross_offset, 0)
    for index, offset in enumerate(offsets):
        row = marks_v[pl.ds(offset + 1, 1), :].astype(jnp.float32)
        marks_t[index] = jnp.broadcast_to(row, (LANES, LANES)).T
        pattern = marks_t[index, pl.ds(inside, blocks), :]
        distance = jnp.asarray(offset, jnp.float32) + position - 0.5
        smooth = jnp.exp(-0.5 * distance * distance)
        weight_v[index] = jnp.where(alive & (pattern > 0), smooth, jnp.zeros_like(smooth))

    def gram(index):
        for c in range(CHUNKS):
            if index == 0:
                obs_copies[c].wait()
            for b in range(c * blocks // CHUNKS, (c + 1) * blocks // CHUNKS):
                columns = pl.ds(b * LANES, LANES)
                weight = weight_v[index, pl.ds(b, 1), :]
                scaled_v[pl.ds(0, members), columns] = (
                    obs_v[pl.ds(0, members), columns].astype(jnp.float32) * weight
                ).astype(jnp.bfloat16)
                innovation = obs_v[pl.ds(members, 1), columns].astype(jnp.float32) * weight
                scaled_v[pl.ds(members, 16), columns] = jnp.broadcast_to(
                    innovation, (16, LANES)
                ).astype(jnp.bfloat16)
        return lax.dot_general(
            scaled_v[...],
            scaled_v[pl.ds(0, members), :],
            (((1,), (1,)), ((), ())),
            preferred_element_type=jnp.float32,
        )

    def packed(products):
        upper = products[:half, :half]
        drive = products[members : members + 1, :]
        left, right = drive[:, :half], drive[:, half:]
        rows = jnp.concatenate(
            [
                left,
                pltpu.roll(left, half // 2, 1),
                right,
                pltpu.roll(right, half // 2, 1),
                jnp.zeros((4, half), jnp.float32),
            ],
            axis=0,
        )
        lane = lax.broadcasted_iota(jnp.int32, (8, half), 1)
        last = jnp.where(lane < half // 2, rows, upper[half - 8 :])
        upper = jnp.concatenate([upper[: half - 8], last], axis=0)
        return [
            block.reshape(n_mem, part, half)
            for block in (upper, products[:half, half:], products[half:members, half:])
        ]

    def put(ref, blocks_of):
        for i, block in enumerate(blocks_of):
            ref[:, pl.ds(i * part, part), :] = block

    put(cross_out, packed(gram(0)))
    pl.semaphore_wait(barrier, n_mem + 1)
    cross = pltpu.make_async_remote_copy(
        cross_out, cross_in, pair_send.at[0], pair_recv.at[0], (cross_tile, mem), MESH
    )
    cross.start()
    put(inner_out, packed(gram(1)))
    inner = pltpu.make_async_remote_copy(
        inner_out, inner_in, pair_send.at[1], pair_recv.at[1], (inner_tile, mem), MESH
    )
    inner.start()
    put(total, packed(gram(2)))
    inner.wait_recv()
    cross.wait_recv()
    total[...] += inner_in[...] + cross_in[...]

    scatter = [
        pltpu.make_async_remote_copy(
            total.at[peer],
            parts_in.at[k],
            rs_send.at[k],
            rs_recv.at[k],
            (tile, peer),
            MESH,
        )
        for k, peer in enumerate(peers)
    ]
    for copy in scatter:
        copy.start()
    mine = total[mem]
    for k, copy in enumerate(scatter):
        copy.wait_recv()
        mine = mine + parts_in[k]
    system_v[mem] = mine
    share = [
        pltpu.make_async_remote_copy(
            system_v.at[mem],
            system_v.at[mem],
            ag_send.at[k],
            ag_recv.at[k],
            (tile, peer),
            MESH,
        )
        for k, peer in enumerate(peers)
    ]
    for copy in share:
        copy.start()

    home = gathered.at[pl.ds(pl.multiple_of(mem * own_rows, own_rows), own_rows), :]

    def cells(owner):
        return prior.at[:, pl.ds(pl.multiple_of(owner * own_cols, own_cols), own_cols)]

    spread = [
        pltpu.make_async_remote_copy(
            cells(peer), home, a2a_send.at[k], a2a_recv.at[k], (tile, peer), MESH
        )
        for k, peer in enumerate(peers)
    ]
    keep = pltpu.make_async_copy(cells(mem), home, local_sem.at[1])
    for copy in spread:
        copy.start()
    keep.start()

    for copy in share:
        copy.wait_recv()
    upper, side, lower = (
        system_v[:, pl.ds(i * part, part), :].reshape(half, half) for i in range(3)
    )
    corner = upper[half - 8 :]
    lane = lax.broadcasted_iota(jnp.int32, (1, half), 1)
    drive = jnp.concatenate(
        [
            jnp.where(lane < half // 2, corner[i : i + 1], pltpu.roll(corner[i + 1 : i + 2], half // 2, 1))
            for i in (0, 2)
        ],
        axis=1,
    )
    above = lax.broadcasted_iota(jnp.int32, (half, half), 1) >= lax.broadcasted_iota(
        jnp.int32, (half, half), 0
    )
    upper = jnp.where(above, upper, upper.T)
    gram_block = jnp.concatenate(
        [
            jnp.concatenate([upper, side], axis=1),
            jnp.concatenate([side.T, lower], axis=1),
        ],
        axis=0,
    )
    diagonal = lax.broadcasted_iota(jnp.int32, (members, members), 0) == lax.broadcasted_iota(
        jnp.int32, (members, members), 1
    )
    identity = diagonal.astype(jnp.float32)
    system = (members - 1.0) * identity + gram_block
    bound = jnp.max(jnp.sum(jnp.abs(system), axis=1, keepdims=True), axis=0, keepdims=True)
    both = system / bound
    inverse_root = None
    for sweep in range(NS_STEPS):
        factor = 1.5 * identity - 0.5 * both
        halves = split(factor)
        if sweep < NS_STEPS - 1:
            once = product(split(both), halves)
        inverse_root = factor if sweep == 0 else product(split(inverse_root), halves)
        if sweep < NS_STEPS - 1:
            both = product(split(once), halves)
    inner_shift = jnp.sum(inverse_root * drive, axis=1, keepdims=True)
    mean_shift = jnp.sum(inverse_root * inner_shift, axis=0, keepdims=True) / bound
    weights = inverse_root * (jnp.sqrt(members - 1.0) * lax.rsqrt(bound)) + mean_shift
    mixing = weights + (1.0 - jnp.sum(weights, axis=1, keepdims=True)) / members
    mixing_out[...] = mixing.astype(jnp.bfloat16)

    keep.wait()
    for copy in spread:
        copy.wait_recv()
    for copy in [cross, inner, *scatter, *share, *spread]:
        copy.wait_send()


def solution(mesh):
    n_tile, n_mem = mesh.shape["tile"], mesh.shape["mem"]

    def local(prior, obs, counts, marks):
        members = obs.shape[0] - 1
        half = members // 2
        obs_dev = obs.shape[1]
        blocks = obs_dev // LANES
        packed_shape = (n_mem, 3 * half // n_mem, half)
        dma = pltpu.SemaphoreType.DMA
        mixing, gathered = pl.pallas_call(
            functools.partial(kernel, n_tile, n_mem),
            out_shape=(
                jax.ShapeDtypeStruct((members, members), jnp.bfloat16),
                jax.ShapeDtypeStruct((members, prior.shape[1] // n_mem), jnp.bfloat16),
            ),
            in_specs=[
                pl.BlockSpec(memory_space=pltpu.SMEM),
                pl.BlockSpec(memory_space=pl.ANY),
                pl.BlockSpec(memory_space=pl.ANY),
                pl.BlockSpec(memory_space=pl.ANY),
            ],
            out_specs=(
                pl.BlockSpec(memory_space=pltpu.VMEM),
                pl.BlockSpec(memory_space=pl.ANY),
            ),
            scratch_shapes=[
                pltpu.VMEM(obs.shape, jnp.bfloat16),
                pltpu.VMEM((3, LANES), jnp.int32),
                pltpu.VMEM((3, LANES, LANES), jnp.float32),
                pltpu.VMEM((3, blocks, LANES), jnp.float32),
                pltpu.VMEM((members + 16, obs_dev), jnp.bfloat16),
                pltpu.VMEM(packed_shape, jnp.float32),
                pltpu.VMEM(packed_shape, jnp.float32),
                pltpu.VMEM(packed_shape, jnp.float32),
                pltpu.VMEM(packed_shape, jnp.float32),
                pltpu.VMEM(packed_shape, jnp.float32),
                pltpu.VMEM((n_mem - 1, *packed_shape[1:]), jnp.float32),
                pltpu.VMEM(packed_shape, jnp.float32),
                dma((2,)),
                dma((CHUNKS,)),
                dma((2,)),
                dma((2,)),
                dma((n_mem - 1,)),
                dma((n_mem - 1,)),
                dma((n_mem - 1,)),
                dma((n_mem - 1,)),
                dma((n_mem - 1,)),
                dma((n_mem - 1,)),
            ],
            compiler_params=pltpu.CompilerParams(
                collective_id=0, has_side_effects=True, vmem_limit_bytes=32 * 1024 * 1024
            ),
        )(counts, prior, obs, marks)
        return jnp.dot(mixing, gathered, preferred_element_type=jnp.float32).astype(jnp.bfloat16)

    placed = (P("mem", "tile"), P(None, ("tile", "mem")), P(), P())
    return jax.shard_map(
        local, mesh=mesh, in_specs=placed, out_specs=P(None, ("tile", "mem")), check_vma=False
    )
```
